32 devices in a mesh: tm: 2 (over x), row: 16 (over z, y, core).
Axes of the slice: x: 2, y: 2, z: 4, core: 2. Of those that a mesh axis runs over, the one named last changes fastest.
Arguments:
- snapshots: float32 [16384, 256], P('row', 'tm'), may hold values from -6 to 6
- sketches: float32 [1, 256, 128], replicated, may hold values from -0.375 to 0.375
Outputs:
- coefficients: float32 [128, 256], P(None, 'tm')
- deflated: float32 [16384, 256], P('row', 'tm')
The draws below stay inside these ranges and needn't reach their ends.
All inputs are finite; a program needn't handle non-finite values.
Results may differ from the reference program's by a relative error of at most 0.00024.
Values sent between devices are 32-bit elements; how exact they have to be, the bound alone decides.
No kernel may reach another device: no remote copies, remote signals or barrier semaphores. Data moves between devices by JAX's collectives and lax.ppermute only.
A program may use at most 64 MiB of HBM per device.

```python
import jax
import jax.numpy as jnp
from jax import lax

MODES = 128
NS_STEPS = 5
ROWS = 16384
SNAPS = 256
LEVELS = 1
N_TM = 2


def level_of(stream_key, extent, shards, low, high):
    level = 1.0
    for axis_at, shards_of in shards:
        draws = jax.random.uniform(jax.random.fold_in(jax.random.fold_in(stream_key, 6), axis_at), (shards_of,), jnp.float32, low / len(shards), high / len(shards))
        level = level * jnp.repeat(jnp.exp(draws), extent[axis_at] // shards_of).reshape((-1,) + (1,) * (len(extent) - 1 - axis_at))
    return level


def noise(stream_key, dims, scale, bound, shards=(), kind=jnp.bfloat16):
    result = jax.random.normal(stream_key, dims, jnp.float32) * scale
    if len(shards) > 0:
        result = level_of(stream_key, dims, shards, -0.22, 0.18) * result
    return jnp.clip(result, min=-bound, max=bound).astype(kind)


def setup_inputs(seed: int = 0) -> dict:
    key_list = jax.random.split(jax.random.key(seed), 3)
    return {
        "snapshots": noise(key_list[0], (ROWS, SNAPS), 1.0, 6.0, ((0, 16), (1, 2)), jnp.float32),
        "sketches": noise(key_list[1], (LEVELS, 2 * MODES, MODES), (2 * MODES) ** -0.5, 0.375, (), jnp.float32),
    }


HIGH = lax.Precision.HIGHEST

def inverse_root(matrix):
    frob_scale = jnp.sqrt(jnp.sum(matrix * matrix) + 1e-06)
    ident = jnp.eye(matrix.shape[0], dtype=matrix.dtype)
    y_iter = matrix / frob_scale
    z_iter = ident
    for repeat in range(NS_STEPS):
        middle = 1.5 * ident - 0.5 * jnp.dot(z_iter, y_iter, precision=HIGH)
        y_iter = jnp.dot(y_iter, middle, precision=HIGH)
        z_iter = jnp.dot(middle, z_iter, precision=HIGH)
    return z_iter / jnp.sqrt(frob_scale)

def reference(snapshots, sketches):
    groups = snapshots.reshape(ROWS, N_TM, MODES).transpose(1, 0, 2)
    grams = jnp.einsum('nrk,nrj->nkj', groups, groups, precision=HIGH)
    roots = jax.vmap(inverse_root)(grams)
    mode_blocks = jnp.einsum('nrk,nkj->nrj', groups, roots, precision=HIGH)
    for tree_level in range(LEVELS):
        earlier = jnp.roll(mode_blocks, 2 ** tree_level, axis=0)
        joined = jnp.concatenate([earlier, mode_blocks], axis=2)
        sketch = sketches[tree_level]
        grams = jnp.einsum('nrk,nrj->nkj', joined, joined, precision=HIGH)
        reduced = jnp.einsum('nkj,jm->nkm', grams, sketch, precision=HIGH)
        temp_prod = jnp.einsum('nkj,njm->nkm', grams, reduced, precision=HIGH)
        small = jnp.einsum('nkm,nkp->nmp', reduced, temp_prod, precision=HIGH)
        roots = jax.vmap(inverse_root)(small)
        mixing = jnp.einsum('nkm,nmp->nkp', reduced, roots, precision=HIGH)
        mode_blocks = jnp.einsum('nrk,nkp->nrp', joined, mixing, precision=HIGH)
    coeff_blocks = jnp.einsum('nrk,nrj->nkj', mode_blocks, groups, precision=HIGH)
    removed = groups - jnp.einsum('nrk,nkj->nrj', mode_blocks, coeff_blocks, precision=HIGH)
    coefficients = coeff_blocks.transpose(1, 0, 2).reshape(MODES, SNAPS)
    deflated = removed.transpose(1, 0, 2).reshape(ROWS, SNAPS)
    return (coefficients, deflated)
```

```python
import jax
import jax.numpy as jnp
from jax import lax
from jax.sharding import PartitionSpec as P

NS_STEPS = 5


HIGH = lax.Precision.HIGH
HIGHEST = lax.Precision.HIGHEST


def passed_along(block, axis, distance):
    devices = range(lax.axis_size(axis))
    route = [((i - distance) % len(devices), i) for i in devices]
    return lax.ppermute(block, axis, route)


def product_t(left, right, precision=HIGHEST):
    return jnp.dot(left.T, right, precision=precision, preferred_element_type=jnp.float32)


def product(left, right, precision=HIGHEST):
    return jnp.dot(left, right, precision=precision, preferred_element_type=jnp.float32)


def stages_of(size):
    bits = [1 << b for b in range(size.bit_length() - 1)]
    stages = [(bits[0],)] if bits else []
    rest = bits[1:]
    while rest:
        stages.append(tuple(rest[:2]) if len(rest) >= 2 else tuple(rest))
        rest = rest[2:]
    return stages


def row_sum(part, axis="row"):
    size = lax.axis_size(axis)
    if size & (size - 1):
        return lax.psum(part, axis)
    for bits in stages_of(size):
        flips = [bits[0]] if len(bits) == 1 else [bits[0], bits[1], bits[0] | bits[1]]
        others = [lax.ppermute(part, axis, [(i, i ^ flip) for i in range(size)]) for flip in flips]
        if len(others) == 1:
            part = part + others[0]
        else:
            part = (part + others[0]) + (others[1] + others[2])
    return part


def inverse_root(matrix):
    frob_scale = jnp.sqrt(jnp.sum(matrix * matrix) + 1e-06)
    ident = jnp.eye(matrix.shape[0], dtype=matrix.dtype)
    y_iter = matrix / frob_scale
    z_iter = ident
    for repeat in range(NS_STEPS):
        if repeat == 0:
            middle = 1.5 * ident - 0.5 * y_iter
            z_iter = middle
        else:
            middle = 1.5 * ident - 0.5 * product(z_iter, y_iter)
            z_iter = product(middle, z_iter)
        y_iter = product(y_iter, middle)
    return z_iter / jnp.sqrt(frob_scale)


def one_merge(snapshots, sketch):
    modes = snapshots.shape[1]
    lower = passed_along(snapshots, "tm", 1)
    own_gram = row_sum(product_t(snapshots, snapshots, HIGH))
    own_root = inverse_root(own_gram)
    lower_gram, lower_root = passed_along((own_gram, own_root), "tm", 1)
    cross = row_sum(product_t(lower, snapshots, HIGH))
    top, bottom = sketch[:modes], sketch[modes:]
    lower_e, own_e = product(lower_root, top), product(own_root, bottom)
    whole = jnp.concatenate(
        [jnp.concatenate([lower_gram, cross], axis=1), jnp.concatenate([cross.T, own_gram], axis=1)], axis=0
    )
    f = product(whole, jnp.concatenate([lower_e, own_e], axis=0))
    v = jnp.concatenate(
        [
            product(lower_root, product_t(lower_root, f[:modes])),
            product(own_root, product_t(own_root, f[modes:])),
        ],
        axis=0,
    )
    p = product(whole, v)
    root = inverse_root(product_t(v, p))
    coefficients = product_t(root, p[modes:].T)
    mixed = product(v, product(root, coefficients))
    deflated = snapshots - product(lower, mixed[:modes], HIGH) - product(snapshots, mixed[modes:], HIGH)
    return coefficients, deflated


def many_merges(snapshots, sketches, tree_depth):
    leaf_sum = row_sum(product_t(snapshots, snapshots))
    leaf_root = inverse_root(leaf_sum)
    mode_block = product(snapshots, leaf_root)
    own_gram = product_t(leaf_root, product(leaf_sum, leaf_root))
    for tree_level in range(tree_depth):
        sketch = sketches[tree_level]
        lower_block, lower_gram = passed_along((mode_block, own_gram), "tm", 1 << tree_level)
        cross_sum = row_sum(product_t(lower_block, mode_block))
        top_rows = jnp.concatenate([lower_gram, cross_sum], axis=1)
        bottom_rows = jnp.concatenate([cross_sum.T, own_gram], axis=1)
        gram_sum = jnp.concatenate([top_rows, bottom_rows], axis=0)
        joined = jnp.concatenate([lower_block, mode_block], axis=1)
        reduced = product(gram_sum, sketch)
        small = product_t(reduced, product(gram_sum, reduced))
        mixing = product(reduced, inverse_root(small))
        mode_block = product(joined, mixing)
        own_gram = product_t(mixing, product(gram_sum, mixing))
    coefficients = row_sum(product_t(mode_block, snapshots))
    deflated = snapshots - product(mode_block, coefficients)
    return coefficients, deflated


def body(snapshots, sketches):
    tree_depth = lax.axis_size("tm").bit_length() - 1
    if tree_depth == 1:
        return one_merge(snapshots, sketches[0])
    return many_merges(snapshots, sketches, tree_depth)


def solution(mesh):
    placed = (P("row", "tm"), P())
    return jax.shard_map(
        body, mesh=mesh, in_specs=placed, out_specs=(P(None, "tm"), P("row", "tm")), check_vma=False
    )
```

```python
import jax
import jax.numpy as jnp
from jax import lax
from jax.experimental import pallas as pl
from jax.experimental.pallas import tpu as pltpu
from jax.sharding import PartitionSpec as P

NS_STEPS = 5
HIGHEST = lax.Precision.HIGHEST
F32 = jnp.float32
BF16 = jnp.bfloat16
IN_VMEM = pl.BlockSpec(memory_space=pltpu.VMEM)
LIMITED = pltpu.CompilerParams(vmem_limit_bytes=12 << 20)
ANYWHERE = pl.BlockSpec(memory_space=pl.ANY)


def split(x):
    high = x.astype(BF16)
    rest = x - high.astype(F32)
    middle = rest.astype(BF16)
    low = (rest - middle.astype(F32)).astype(BF16)
    return high, middle, low


def dot(left, right):
    return jnp.dot(left, right, preferred_element_type=F32)


def dot_t(left, right):
    return lax.dot_general(left, right, (((0,), (0,)), ((), ())), preferred_element_type=F32)


def mul(left, right):
    lh, lm, ll = left
    rh, rm, rl = right
    n = rh.shape[1]
    both = jnp.concatenate([jnp.concatenate([rh, rm], 1), jnp.concatenate([rm, rh], 1)], 0)
    wide = dot(jnp.concatenate([lh, lm], 1), both)
    small = dot(jnp.concatenate([ll, lh], 1), jnp.concatenate([rh, rl], 0))
    return wide[:, :n] + (wide[:, n:] + small)


def mul_t(left, right):
    lh, lm, ll = left
    rh, rm, rl = right
    k, n = lh.shape[1], rh.shape[1]
    wide = dot_t(jnp.concatenate([lh, lm, ll], 1), jnp.concatenate([rh, rm], 1))
    small = dot_t(lh, rl)
    return wide[:k, :n] + ((wide[:k, n:] + wide[k : 2 * k, :n]) + (wide[k : 2 * k, n:] + (wide[2 * k :, :n] + small)))


def mul_long(left, right):
    lh, lm, ll = left
    rh, rm, rl = right
    n = rh.shape[1]
    both = jnp.concatenate([rh, rm], 1)
    first, second = dot(lh, both), dot(lm, both)
    return first[:, :n] + ((first[:, n:] + second[:, :n]) + (second[:, n:] + (dot(ll, rh) + dot(lh, rl))))


def identity(size):
    return (
        lax.broadcasted_iota(jnp.int32, (size, size), 0) == lax.broadcasted_iota(jnp.int32, (size, size), 1)
    ).astype(F32)


def root_iteration(matrices):
    eye = identity(matrices[0].shape[0])
    squares = []
    for a in matrices:
        parts = split(a)
        squares.append(mul(parts, parts))
    scales = [jnp.sqrt(jnp.sum(a * a, keepdims=True) + 1e-06) for a in matrices]
    ys, zs = [], []
    for a, square, scale in zip(matrices, squares, scales):
        inverse = 1.0 / scale
        y = a * inverse
        ys.append(1.5 * y - (0.5 * inverse * inverse) * square)
        zs.append(1.5 * eye - 0.5 * y)
    for repeat in range(1, NS_STEPS):
        y_parts, z_parts = [split(y) for y in ys], [split(z) for z in zs]
        middles = [1.5 * eye - 0.5 * mul(z, y) for z, y in zip(z_parts, y_parts)]
        if repeat == NS_STEPS - 1:
            return zs, middles, scales
        m_parts = [split(m) for m in middles]
        ys = [mul(y, m) for y, m in zip(y_parts, m_parts)]
        zs = [mul(m, z) for z, m in zip(z_parts, m_parts)]


def gram_kernel(x_ref, out_ref):
    parts = split(x_ref[...])
    k = x_ref.shape[1]
    h, m, l = parts
    wide = dot_t(jnp.concatenate([h, m, l], 1), jnp.concatenate([h, m], 1))
    cross = wide[:k, k:] + wide[2 * k :, :k]
    out_ref[...] = (wide[:k, :k] + wide[k : 2 * k, k:]) + (cross + cross.T)


def cross_kernel(left_ref, right_ref, out_ref):
    out_ref[...] = mul_t(split(left_ref[...]), split(right_ref[...]))


def leaf_kernel(lower_ref, own_ref, sketch_ref, e_ref, m_ref, f_ref, hm_ref):
    n = own_ref.shape[0]
    grams = [lower_ref[...], own_ref[...]]
    zs, middles, scales = root_iteration(grams)
    roots = [mul(split(m), split(z)) * lax.rsqrt(c) for z, m, c in zip(zs, middles, scales)]
    for at, (gram, root) in enumerate(zip(grams, roots)):
        rows = slice(at * n, (at + 1) * n)
        root_parts, gram_parts = split(root), split(gram)
        e = mul(root_parts, split(sketch_ref[rows, :]))
        m = mul(root_parts, split(root.T))
        e_ref[rows, :] = e
        m_ref[rows, :] = m
        f_ref[rows, :] = mul(gram_parts, split(e))
        hm_ref[rows, :] = mul(gram_parts, split(m))


def merge_kernel(cross_ref, e_ref, m_ref, f_ref, hm_ref, lower_ref, own_ref, coef_ref, out_ref, stage_ref, sems):
    n = cross_ref.shape[0]
    low, own = slice(0, n), slice(n, 2 * n)
    cross = cross_ref[...]
    cross_parts, cross_t_parts = split(cross), split(cross.T)
    e_low, e_own = split(e_ref[low, :]), split(e_ref[own, :])
    m_low, m_own = split(m_ref[low, :]), split(m_ref[own, :])
    right = mul(cross_parts, [jnp.concatenate([a, b], 1) for a, b in zip(e_own, m_own)])
    left = mul(cross_t_parts, [jnp.concatenate([a, b], 1) for a, b in zip(e_low, m_low)])
    f = jnp.concatenate([f_ref[low, :] + right[:, :n], f_ref[own, :] + left[:, :n]], 0)
    f_parts = split(f)
    hm = jnp.concatenate(
        [jnp.concatenate([hm_ref[low, :], right[:, n:]], 1), jnp.concatenate([left[:, n:], hm_ref[own, :]], 1)], 0
    )
    p = mul_long(split(hm), f_parts)
    v = jnp.concatenate([mul(m_low, [q[:n] for q in f_parts]), mul(m_own, [q[n:] for q in f_parts])], 0)
    small = mul_t(split(v), split(p))
    (z,), (middle,), (scale,) = root_iteration([small])
    both = mul(split(jnp.concatenate([v, p[n:]], 0)), split(z))
    both = mul(split(both), split(middle)) * lax.rsqrt(scale)
    coefficients = both[2 * n :].T
    coef_ref[...] = coefficients
    mixed = split(mul(split(both[: 2 * n]), split(coefficients)))
    rows, chunks = own_ref.shape[0], sems.shape[0]
    step = rows // chunks
    copies = []
    for at in range(chunks):
        here = slice(at * step, (at + 1) * step)
        x = own_ref[here, :]
        joined = split(jnp.concatenate([lower_ref[here, :], x], 1))
        stage_ref[here, :] = x - mul_long(joined, mixed)
        copy = pltpu.make_async_copy(stage_ref.at[here], out_ref.at[here], sems.at[at])
        copy.start()
        copies.append(copy)
    for copy in copies:
        copy.wait()


def shape(*dims):
    return jax.ShapeDtypeStruct(dims, F32)


def cost(flops, count):
    return pl.CostEstimate(flops=flops, bytes_accessed=count, transcendentals=0)


def passed_along(block, axis, distance):
    devices = range(lax.axis_size(axis))
    route = [((i - distance) % len(devices), i) for i in devices]
    return lax.ppermute(block, axis, route)


def stages_of(size):
    bits = [1 << b for b in range(size.bit_length() - 1)]
    stages, rest = [(b,) for b in bits[:1]], bits[1:]
    while rest:
        stages.append(tuple(rest[:2]))
        rest = rest[2:]
    return stages


def summed_over(part, axis, bits):
    size = lax.axis_size(axis)
    flips = [bits[0]] if len(bits) == 1 else [bits[0], bits[1], bits[0] | bits[1]]
    others = [lax.ppermute(part, axis, [(i, i ^ flip) for i in range(size)]) for flip in flips]
    if len(others) == 1:
        return part + others[0]
    return (part + others[0]) + (others[1] + others[2])


def row_sum(part, axis="row"):
    size = lax.axis_size(axis)
    if size & (size - 1):
        return lax.psum(part, axis)
    for bits in stages_of(size):
        part = summed_over(part, axis, bits)
    return part


def one_merge(snapshots, sketch):
    rows, n = snapshots.shape
    lower = passed_along(snapshots, "tm", 1)
    gram = pl.pallas_call(
        gram_kernel, out_shape=shape(n, n), in_specs=[IN_VMEM], out_specs=IN_VMEM, name="own_gram",
        compiler_params=LIMITED,
    )(snapshots)
    own_gram = row_sum(gram)
    own_gram, lower = lax.optimization_barrier((own_gram, lower))
    cross = pl.pallas_call(
        cross_kernel, out_shape=shape(n, n), in_specs=[IN_VMEM] * 2, out_specs=IN_VMEM, name="cross_gram",
        compiler_params=LIMITED,
    )(lower, snapshots)
    lower_gram = passed_along(own_gram, "tm", 1)
    leaf = pl.pallas_call(
        leaf_kernel,
        out_shape=[shape(2 * n, n)] * 4,
        in_specs=[IN_VMEM] * 3,
        out_specs=[IN_VMEM] * 4,
        compiler_params=LIMITED,
        name="leaf_roots",
    )(lower_gram, own_gram, sketch)
    cross = row_sum(cross)
    chunks = 4
    coefficients, deflated = pl.pallas_call(
        merge_kernel,
        out_shape=[shape(n, n), shape(rows, n)],
        in_specs=[IN_VMEM] * 7,
        out_specs=[IN_VMEM, ANYWHERE],
        scratch_shapes=[pltpu.VMEM((rows, n), F32), pltpu.SemaphoreType.DMA((chunks,))],
        compiler_params=LIMITED,
        name="merge",
    )(cross, *leaf, lower, snapshots)
    return coefficients, deflated


def product_t(left, right):
    return jnp.dot(left.T, right, precision=HIGHEST, preferred_element_type=F32)


def product(left, right):
    return jnp.dot(left, right, precision=HIGHEST, preferred_element_type=F32)


def inverse_root(matrix):
    frob_scale = jnp.sqrt(jnp.sum(matrix * matrix) + 1e-06)
    ident = jnp.eye(matrix.shape[0], dtype=matrix.dtype)
    y_iter = matrix / frob_scale
    z_iter = ident
    for repeat in range(NS_STEPS):
        middle = 1.5 * ident - 0.5 * product(z_iter, y_iter)
        y_iter = product(y_iter, middle)
        z_iter = product(middle, z_iter)
    return z_iter / jnp.sqrt(frob_scale)


def many_merges(snapshots, sketches, tree_depth):
    leaf_sum = row_sum(product_t(snapshots, snapshots))
    leaf_root = inverse_root(leaf_sum)
    mode_block = product(snapshots, leaf_root)
    own_gram = product_t(leaf_root, product(leaf_sum, leaf_root))
    for tree_level in range(tree_depth):
        sketch = sketches[tree_level]
        lower_block, lower_gram = passed_along((mode_block, own_gram), "tm", 1 << tree_level)
        cross_sum = row_sum(product_t(lower_block, mode_block))
        top_rows = jnp.concatenate([lower_gram, cross_sum], axis=1)
        bottom_rows = jnp.concatenate([cross_sum.T, own_gram], axis=1)
        gram_sum = jnp.concatenate([top_rows, bottom_rows], axis=0)
        joined = jnp.concatenate([lower_block, mode_block], axis=1)
        reduced = product(gram_sum, sketch)
        small = product_t(reduced, product(gram_sum, reduced))
        mixing = product(reduced, inverse_root(small))
        mode_block = product(joined, mixing)
        own_gram = product_t(mixing, product(gram_sum, mixing))
    coefficients = row_sum(product_t(mode_block, snapshots))
    deflated = snapshots - product(mode_block, coefficients)
    return coefficients, deflated


def body(snapshots, sketches):
    tree_depth = lax.axis_size("tm").bit_length() - 1
    if tree_depth == 1:
        return one_merge(snapshots, sketches[0])
    return many_merges(snapshots, sketches, tree_depth)


def solution(mesh):
    placed = (P("row", "tm"), P())
    return jax.shard_map(
        body, mesh=mesh, in_specs=placed, out_specs=(P(None, "tm"), P("row", "tm")), check_vma=False
    )
```

```python
import jax
import jax.numpy as jnp
from jax import lax
from jax.experimental import pallas as pl
from jax.experimental.pallas import tpu as pltpu
from jax.sharding import PartitionSpec as P

NS_STEPS = 5
HIGHEST = lax.Precision.HIGHEST
F32 = jnp.float32
BF16 = jnp.bfloat16
IN_VMEM = pl.BlockSpec(memory_space=pltpu.VMEM)
LIMITED = pltpu.CompilerParams(vmem_limit_bytes=12 << 20)
ANYWHERE = pl.BlockSpec(memory_space=pl.ANY)


def split(x):
    high = x.astype(BF16)
    rest = x - high.astype(F32)
    middle = rest.astype(BF16)
    low = (rest - middle.astype(F32)).astype(BF16)
    return high, middle, low


def dot(left, right):
    return jnp.dot(left, right, preferred_element_type=F32)


def dot_t(left, right):
    return lax.dot_general(left, right, (((0,), (0,)), ((), ())), preferred_element_type=F32)


def mul(left, right):
    lh, lm, ll = left
    rh, rm, rl = right
    n = rh.shape[1]
    both = jnp.concatenate([jnp.concatenate([rh, rm], 1), jnp.concatenate([rm, rh], 1)], 0)
    wide = dot(jnp.concatenate([lh, lm], 1), both)
    small = dot(jnp.concatenate([ll, lh], 1), jnp.concatenate([rh, rl], 0))
    return wide[:, :n] + (wide[:, n:] + small)


def mul_t(left, right):
    lh, lm, ll = left
    rh, rm, rl = right
    k, n = lh.shape[1], rh.shape[1]
    wide = dot_t(jnp.concatenate([lh, lm, ll], 1), jnp.concatenate([rh, rm], 1))
    small = dot_t(lh, rl)
    return wide[:k, :n] + ((wide[:k, n:] + wide[k : 2 * k, :n]) + (wide[k : 2 * k, n:] + (wide[2 * k :, :n] + small)))


def mul_long(left, right):
    lh, lm, ll = left
    rh, rm, rl = right
    n = rh.shape[1]
    both = jnp.concatenate([rh, rm], 1)
    first, second = dot(lh, both), dot(lm, both)
    return first[:, :n] + ((first[:, n:] + second[:, :n]) + (second[:, n:] + (dot(ll, rh) + dot(lh, rl))))


def identity(size):
    return (
        lax.broadcasted_iota(jnp.int32, (size, size), 0) == lax.broadcasted_iota(jnp.int32, (size, size), 1)
    ).astype(F32)


def root_iteration(matrices):
    eye = identity(matrices[0].shape[0])
    squares = []
    for a in matrices:
        parts = split(a)
        squares.append(mul(parts, parts))
    scales = [jnp.sqrt(jnp.sum(a * a, keepdims=True) + 1e-06) for a in matrices]
    ys, zs = [], []
    for a, square, scale in zip(matrices, squares, scales):
        inverse = 1.0 / scale
        y = a * inverse
        ys.append(1.5 * y - (0.5 * inverse * inverse) * square)
        zs.append(1.5 * eye - 0.5 * y)
    for repeat in range(1, NS_STEPS):
        y_parts, z_parts = [split(y) for y in ys], [split(z) for z in zs]
        middles = [1.5 * eye - 0.5 * mul(z, y) for z, y in zip(z_parts, y_parts)]
        if repeat == NS_STEPS - 1:
            return zs, middles, scales
        m_parts = [split(m) for m in middles]
        ys = [mul(y, m) for y, m in zip(y_parts, m_parts)]
        zs = [mul(m, z) for z, m in zip(z_parts, m_parts)]


def gram_kernel(x_ref, out_ref):
    parts = split(x_ref[...])
    k = x_ref.shape[1]
    h, m, l = parts
    wide = dot_t(jnp.concatenate([h, m, l], 1), jnp.concatenate([h, m], 1))
    cross = wide[:k, k:] + wide[2 * k :, :k]
    out_ref[...] = (wide[:k, :k] + wide[k : 2 * k, k:]) + (cross + cross.T)


def cross_kernel(left_ref, right_ref, out_ref):
    out_ref[...] = mul_t(split(left_ref[...]), split(right_ref[...]))


def leaf_kernel(lower_ref, own_ref, sketch_ref, e_ref, m_ref, f_ref, hm_ref):
    n = own_ref.shape[0]
    grams = [lower_ref[...], own_ref[...]]
    zs, middles, scales = root_iteration(grams)
    roots = [mul(split(m), split(z)) * lax.rsqrt(c) for z, m, c in zip(zs, middles, scales)]
    for at, (gram, root) in enumerate(zip(grams, roots)):
        rows = slice(at * n, (at + 1) * n)
        root_parts, gram_parts = split(root), split(gram)
        e = mul(root_parts, split(sketch_ref[rows, :]))
        m = mul(root_parts, split(root.T))
        e_ref[rows, :] = e
        m_ref[rows, :] = m
        f_ref[rows, :] = mul(gram_parts, split(e))
        hm_ref[rows, :] = mul(gram_parts, split(m))


def merge_kernel(cross_ref, e_ref, m_ref, f_ref, hm_ref, lower_ref, own_ref, coef_ref, out_ref, stage_ref, sems):
    n = cross_ref.shape[0]
    low, own = slice(0, n), slice(n, 2 * n)
    cross = cross_ref[...]
    cross_parts, cross_t_parts = split(cross), split(cross.T)
    e_low, e_own = split(e_ref[low, :]), split(e_ref[own, :])
    m_low, m_own = split(m_ref[low, :]), split(m_ref[own, :])
    right = mul(cross_parts, [jnp.concatenate([a, b], 1) for a, b in zip(e_own, m_own)])
    left = mul(cross_t_parts, [jnp.concatenate([a, b], 1) for a, b in zip(e_low, m_low)])
    f = jnp.concatenate([f_ref[low, :] + right[:, :n], f_ref[own, :] + left[:, :n]], 0)
    f_parts = split(f)
    hm = jnp.concatenate(
        [jnp.concatenate([hm_ref[low, :], right[:, n:]], 1), jnp.concatenate([left[:, n:], hm_ref[own, :]], 1)], 0
    )
    p = mul_long(split(hm), f_parts)
    v = jnp.concatenate([mul(m_low, [q[:n] for q in f_parts]), mul(m_own, [q[n:] for q in f_parts])], 0)
    small = mul_t(split(v), split(p))
    (z,), (middle,), (scale,) = root_iteration([small])
    both = mul(split(jnp.concatenate([v, p[n:]], 0)), split(z))
    both = mul(split(both), split(middle)) * lax.rsqrt(scale)
    coefficients = both[2 * n :].T
    coef_ref[...] = coefficients
    mixed = split(mul(split(both[: 2 * n]), split(coefficients)))
    rows, chunks = own_ref.shape[0], sems.shape[0]
    step = rows // chunks
    copies = []
    for at in range(chunks):
        here = slice(at * step, (at + 1) * step)
        x = own_ref[here, :]
        joined = split(jnp.concatenate([lower_ref[here, :], x], 1))
        stage_ref[here, :] = x - mul_long(joined, mixed)
        copy = pltpu.make_async_copy(stage_ref.at[here], out_ref.at[here], sems.at[at])
        copy.start()
        copies.append(copy)
    for copy in copies:
        copy.wait()


def shape(*dims):
    return jax.ShapeDtypeStruct(dims, F32)


def cost(flops, count):
    return pl.CostEstimate(flops=flops, bytes_accessed=count, transcendentals=0)


def passed_along(block, axis, distance):
    devices = range(lax.axis_size(axis))
    route = [((i - distance) % len(devices), i) for i in devices]
    return lax.ppermute(block, axis, route)


def stages_of(size):
    bits = [1 << b for b in range(size.bit_length() - 1)]
    stages, rest = [(b,) for b in bits[:1]], bits[1:]
    while rest:
        stages.append(tuple(rest[:2]))
        rest = rest[2:]
    return stages


def received(part, axis, bits):
    flips = [bits[0]] if len(bits) == 1 else [bits[0], bits[1], bits[0] | bits[1]]
    size = lax.axis_size(axis)
    return [lax.ppermute(part, axis, [(i, i ^ flip) for i in range(size)]) for flip in flips]


def total(part, others):
    if len(others) == 1:
        return part + others[0]
    return (part + others[0]) + (others[1] + others[2])


def summed_over(part, axis, bits):
    return total(part, received(part, axis, bits))


def row_sum(part, axis="row"):
    size = lax.axis_size(axis)
    if size & (size - 1):
        return lax.psum(part, axis)
    for bits in stages_of(size):
        part = summed_over(part, axis, bits)
    return part


def one_merge(snapshots, sketch):
    rows, n = snapshots.shape
    lower = passed_along(snapshots, "tm", 1)
    gram = pl.pallas_call(
        gram_kernel, out_shape=shape(n, n), in_specs=[IN_VMEM], out_specs=IN_VMEM, name="own_gram",
        compiler_params=LIMITED,
    )(snapshots)
    stages = stages_of(lax.axis_size("row"))
    for bits in stages[1:-1]:
        gram = summed_over(gram, "row", bits)
    gram = summed_over(gram, "row", stages[-1])
    own_gram = summed_over(gram, "row", stages[0])
    cross = pl.pallas_call(
        cross_kernel, out_shape=shape(n, n), in_specs=[IN_VMEM] * 2, out_specs=IN_VMEM, name="cross_gram",
        compiler_params=LIMITED,
    )(lower, snapshots)
    cross = summed_over(cross, "row", stages[0])
    lower_gram = passed_along(own_gram, "tm", 1)
    leaf = pl.pallas_call(
        leaf_kernel,
        out_shape=[shape(2 * n, n)] * 4,
        in_specs=[IN_VMEM] * 3,
        out_specs=[IN_VMEM] * 4,
        compiler_params=LIMITED,
        name="leaf_roots",
    )(lower_gram, own_gram, sketch)
    for bits in stages[1:]:
        cross = summed_over(cross, "row", bits)
    chunks = 4
    coefficients, deflated = pl.pallas_call(
        merge_kernel,
        out_shape=[shape(n, n), shape(rows, n)],
        in_specs=[IN_VMEM] * 7,
        out_specs=[IN_VMEM, ANYWHERE],
        scratch_shapes=[pltpu.VMEM((rows, n), F32), pltpu.SemaphoreType.DMA((chunks,))],
        compiler_params=LIMITED,
        name="merge",
    )(cross, *leaf, lower, snapshots)
    return coefficients, deflated


def product_t(left, right):
    return jnp.dot(left.T, right, precision=HIGHEST, preferred_element_type=F32)


def product(left, right):
    return jnp.dot(left, right, precision=HIGHEST, preferred_element_type=F32)


def inverse_root(matrix):
    frob_scale = jnp.sqrt(jnp.sum(matrix * matrix) + 1e-06)
    ident = jnp.eye(matrix.shape[0], dtype=matrix.dtype)
    y_iter = matrix / frob_scale
    z_iter = ident
    for repeat in range(NS_STEPS):
        middle = 1.5 * ident - 0.5 * product(z_iter, y_iter)
        y_iter = product(y_iter, middle)
        z_iter = product(middle, z_iter)
    return z_iter / jnp.sqrt(frob_scale)


def many_merges(snapshots, sketches, tree_depth):
    leaf_sum = row_sum(product_t(snapshots, snapshots))
    leaf_root = inverse_root(leaf_sum)
    mode_block = product(snapshots, leaf_root)
    own_gram = product_t(leaf_root, product(leaf_sum, leaf_root))
    for tree_level in range(tree_depth):
        sketch = sketches[tree_level]
        lower_block, lower_gram = passed_along((mode_block, own_gram), "tm", 1 << tree_level)
        cross_sum = row_sum(product_t(lower_block, mode_block))
        top_rows = jnp.concatenate([lower_gram, cross_sum], axis=1)
        bottom_rows = jnp.concatenate([cross_sum.T, own_gram], axis=1)
        gram_sum = jnp.concatenate([top_rows, bottom_rows], axis=0)
        joined = jnp.concatenate([lower_block, mode_block], axis=1)
        reduced = product(gram_sum, sketch)
        small = product_t(reduced, product(gram_sum, reduced))
        mixing = product(reduced, inverse_root(small))
        mode_block = product(joined, mixing)
        own_gram = product_t(mixing, product(gram_sum, mixing))
    coefficients = row_sum(product_t(mode_block, snapshots))
    deflated = snapshots - product(mode_block, coefficients)
    return coefficients, deflated


def body(snapshots, sketches):
    tree_depth = lax.axis_size("tm").bit_length() - 1
    if tree_depth == 1:
        return one_merge(snapshots, sketches[0])
    return many_merges(snapshots, sketches, tree_depth)


def solution(mesh):
    placed = (P("row", "tm"), P())
    return jax.shard_map(
        body, mesh=mesh, in_specs=placed, out_specs=(P(None, "tm"), P("row", "tm")), check_vma=False
    )
```

```python
import jax
import jax.numpy as jnp
from jax import lax
from jax.experimental import pallas as pl
from jax.experimental.pallas import tpu as pltpu
from jax.sharding import PartitionSpec as P

NS_STEPS = 5
HIGHEST = lax.Precision.HIGHEST
F32 = jnp.float32
BF16 = jnp.bfloat16
IN_VMEM = pl.BlockSpec(memory_space=pltpu.VMEM)
LIMITED = pltpu.CompilerParams(vmem_limit_bytes=12 << 20)
ANYWHERE = pl.BlockSpec(memory_space=pl.ANY)


def split(x):
    high = x.astype(BF16)
    rest = x - high.astype(F32)
    middle = rest.astype(BF16)
    low = (rest - middle.astype(F32)).astype(BF16)
    return high, middle, low


def dot(left, right):
    return jnp.dot(left, right, preferred_element_type=F32)


def dot_t(left, right):
    return lax.dot_general(left, right, (((0,), (0,)), ((), ())), preferred_element_type=F32)


def mul(left, right):
    lh, lm, ll = left
    rh, rm, rl = right
    n = rh.shape[1]
    both = jnp.concatenate([jnp.concatenate([rh, rm], 1), jnp.concatenate([rm, rh], 1)], 0)
    wide = dot(jnp.concatenate([lh, lm], 1), both)
    small = dot(jnp.concatenate([ll, lh], 1), jnp.concatenate([rh, rl], 0))
    return wide[:, :n] + (wide[:, n:] + small)


def mul_t(left, right):
    lh, lm, ll = left
    rh, rm, rl = right
    k, n = lh.shape[1], rh.shape[1]
    wide = dot_t(jnp.concatenate([lh, lm, ll], 1), jnp.concatenate([rh, rm], 1))
    small = dot_t(lh, rl)
    return wide[:k, :n] + ((wide[:k, n:] + wide[k : 2 * k, :n]) + (wide[k : 2 * k, n:] + (wide[2 * k :, :n] + small)))


def identity(size):
    return (
        lax.broadcasted_iota(jnp.int32, (size, size), 0) == lax.broadcasted_iota(jnp.int32, (size, size), 1)
    ).astype(F32)


def root_iteration(matrices):
    eye = identity(matrices[0].shape[0])
    squares = []
    for a in matrices:
        parts = split(a)
        squares.append(mul(parts, parts))
    scales = [jnp.sqrt(jnp.sum(a * a, keepdims=True) + 1e-06) for a in matrices]
    ys, zs = [], []
    for a, square, scale in zip(matrices, squares, scales):
        inverse = 1.0 / scale
        y = a * inverse
        ys.append(1.5 * y - (0.5 * inverse * inverse) * square)
        zs.append(1.5 * eye - 0.5 * y)
    for repeat in range(1, NS_STEPS):
        y_parts, z_parts = [split(y) for y in ys], [split(z) for z in zs]
        middles = [1.5 * eye - 0.5 * mul(z, y) for z, y in zip(z_parts, y_parts)]
        if repeat == NS_STEPS - 1:
            return zs, middles, scales
        m_parts = [split(m) for m in middles]
        ys = [mul(y, m) for y, m in zip(y_parts, m_parts)]
        zs = [mul(m, z) for z, m in zip(z_parts, m_parts)]


def gram_kernel(x_ref, out_ref, buffer_ref, sems):
    k = x_ref.shape[1]
    chunks = sems.shape[0]
    step = x_ref.shape[0] // chunks
    slices = [slice(at * step, (at + 1) * step) for at in range(chunks)]
    copies = [pltpu.make_async_copy(x_ref.at[s], buffer_ref.at[s], sems.at[at]) for at, s in enumerate(slices)]
    for copy in copies:
        copy.start()
    wide = None
    for s, copy in zip(slices, copies):
        copy.wait()
        h, m, l = split(buffer_ref[s, :])
        piece = dot_t(jnp.concatenate([h, m, l], 1), jnp.concatenate([h, m], 1))
        wide = piece if wide is None else wide + piece
    cross = wide[:k, k:] + wide[2 * k :, :k]
    out_ref[...] = (wide[:k, :k] + wide[k : 2 * k, k:]) + (cross + cross.T)


def upper_half():
    return lax.rem(lax.axis_index("row"), 2) == 1


def cross_kernel(left_ref, right_ref, mine_ref, theirs_ref):
    gram = mul_t(split(left_ref[...]), split(right_ref[...]))
    half = gram.shape[0] // 2
    upper = upper_half()
    mine_ref[...] = jnp.where(upper, gram[half:], gram[:half])
    theirs_ref[...] = jnp.where(upper, gram[:half], gram[half:])


def packed(parts):
    high, middle, low = parts
    return jnp.concatenate([high, middle], 1), jnp.concatenate([low, high], 1)


def weights(parts):
    high, middle, low = parts
    both = jnp.concatenate([jnp.concatenate([high, middle], 1), jnp.concatenate([middle, high], 1)], 0)
    return both, jnp.concatenate([high, low], 0)


def mul_packed(left, right):
    n = right[1].shape[1]
    wide = dot(left[0], right[0])
    return wide[:, :n] + (wide[:, n:] + dot(left[1], right[1]))


def split_kernel(lower_ref, own_ref, high_ref, middle_ref, low_ref):
    n = own_ref.shape[1]
    for at, ref in enumerate((lower_ref, own_ref)):
        columns = slice(at * n, (at + 1) * n)
        high_ref[:, columns], middle_ref[:, columns], low_ref[:, columns] = split(ref[...])


def leaf_kernel(lower_ref, own_ref, sketch_ref, f_ref, wide_ref, small_ref, left_ref):
    n = own_ref.shape[0]
    grams = [lower_ref[...], own_ref[...]]
    zs, middles, scales = root_iteration(grams)
    roots = [mul(split(m), split(z)) * lax.rsqrt(c) for z, m, c in zip(zs, middles, scales)]
    for at, (gram, root) in enumerate(zip(grams, roots)):
        rows = slice(at * n, (at + 1) * n)
        root_parts, gram_parts = split(root), split(gram)
        e = split(mul(root_parts, split(sketch_ref[rows, :])))
        m = split(mul(root_parts, split(root.T)))
        wide_ref[at], small_ref[at] = weights([jnp.concatenate([a, b], 1) for a, b in zip(e, m)])
        f_ref[rows, :] = mul(gram_parts, e)
        left_ref[at, 0, :n], left_ref[at, 1, :n] = packed(m)
        left_ref[at, 0, n:], left_ref[at, 1, n:] = packed(split(mul(gram_parts, m)))


def merge_kernel(
    mine_ref, theirs_ref, f_ref, wide_ref, small_ref, left_ref, high_ref, middle_ref, low_ref, own_ref,
    coef_ref, out_ref, coef_stage_ref, stage_ref, coef_sem, sems,
):
    n = mine_ref.shape[1]
    upper = upper_half()
    mine, theirs = mine_ref[...], theirs_ref[...]
    cross = jnp.concatenate([jnp.where(upper, theirs, mine), jnp.where(upper, mine, theirs)], 0)
    right = mul_packed(packed(split(cross)), (wide_ref[1], small_ref[1]))
    left = mul_packed(packed(split(cross.T)), (wide_ref[0], small_ref[0]))
    results = []
    for at, part, other in ((0, right, left), (1, left, right)):
        f = weights(split(f_ref[at * n : (at + 1) * n, :] + part[:, :n]))
        extra = packed(split(other[:, n:]))
        lefts = [jnp.concatenate([left_ref[at, k], extra[k]], 0) for k in range(2)]
        results.append(mul_packed(lefts, f))
    lower, own = results
    v = jnp.concatenate([lower[:n], own[:n]], 0)
    p = jnp.concatenate([lower[n : 2 * n] + own[2 * n :], lower[2 * n :] + own[n : 2 * n]], 0)
    (z,), (middle,), (scale,) = root_iteration([mul_t(split(v), split(p))])
    both = mul(split(jnp.concatenate([v, p[n:]], 0)), split(z))
    both = mul(split(both), split(middle)) * lax.rsqrt(scale)
    coefficients = both[2 * n :].T
    coef_stage_ref[...] = coefficients
    coef_copy = pltpu.make_async_copy(coef_stage_ref, coef_ref, coef_sem)
    coef_copy.start()
    mixed = split(mul(split(both[: 2 * n]), split(coefficients)))
    mixed_both = jnp.concatenate(mixed[:2], 1)
    rows, chunks = own_ref.shape[0], sems.shape[0]
    step = rows // chunks
    copies = []
    for at in range(chunks):
        here = slice(at * step, (at + 1) * step)
        high = high_ref[here, :]
        first, second = dot(high, mixed_both), dot(middle_ref[here, :], mixed_both)
        third = dot(low_ref[here, :], mixed[0]) + dot(high, mixed[2])
        stage_ref[here, :] = own_ref[here, :] - (
            first[:, :n] + ((first[:, n:] + second[:, :n]) + (second[:, n:] + third))
        )
        copy = pltpu.make_async_copy(stage_ref.at[here], out_ref.at[here], sems.at[at])
        copy.start()
        copies.append(copy)
    for copy in copies:
        copy.wait()
    coef_copy.wait()


def shape(*dims, kind=F32):
    return jax.ShapeDtypeStruct(dims, kind)


def passed_along(block, axis, distance):
    devices = range(lax.axis_size(axis))
    route = [((i - distance) % len(devices), i) for i in devices]
    return lax.ppermute(block, axis, route)


def stages_of(size):
    bits = [1 << b for b in range(size.bit_length() - 1)]
    stages, rest = [(b,) for b in bits[:1]], bits[1:]
    while rest:
        stages.append(tuple(rest[:2]))
        rest = rest[2:]
    return stages


def received(part, axis, bits):
    flips = [bits[0]] if len(bits) == 1 else [bits[0], bits[1], bits[0] | bits[1]]
    size = lax.axis_size(axis)
    return [lax.ppermute(part, axis, [(i, i ^ flip) for i in range(size)]) for flip in flips]


def total(part, others):
    if len(others) == 1:
        return part + others[0]
    return (part + others[0]) + (others[1] + others[2])


def summed_over(part, axis, bits):
    return total(part, received(part, axis, bits))


def row_sum(part, axis="row"):
    size = lax.axis_size(axis)
    if size & (size - 1):
        return lax.psum(part, axis)
    for bits in stages_of(size):
        part = summed_over(part, axis, bits)
    return part


def call(kernel, name, outs, **more):
    return pl.pallas_call(kernel, out_shape=outs, compiler_params=LIMITED, name=name, **more)


def one_merge(snapshots, sketch):
    rows, n = snapshots.shape
    lower = passed_along(snapshots, "tm", 1)
    stages = stages_of(lax.axis_size("row"))
    gram = call(
        gram_kernel,
        "own_gram",
        shape(n, n),
        in_specs=[pl.BlockSpec(memory_space=pltpu.HBM)],
        out_specs=IN_VMEM,
        scratch_shapes=[pltpu.VMEM((rows, n), F32), pltpu.SemaphoreType.DMA((2,))],
    )(pltpu.with_memory_space_constraint(snapshots, pltpu.HBM))
    for bits in stages[1:-1]:
        gram = summed_over(gram, "row", bits)
    mine, theirs = call(
        cross_kernel, "cross_gram", [shape(n // 2, n)] * 2, in_specs=[IN_VMEM] * 2, out_specs=[IN_VMEM] * 2
    )(lower, snapshots)
    parts = call(
        split_kernel, "raw_parts", [shape(rows, 2 * n, kind=BF16)] * 3, in_specs=[IN_VMEM] * 2, out_specs=[IN_VMEM] * 3
    )(lower, snapshots)
    others = received(theirs, "row", stages[0])
    others, parts = lax.optimization_barrier((others, parts))
    mine = total(mine, others)
    others, _ = lax.optimization_barrier((received(gram, "row", stages[-1]), mine))
    own_gram = summed_over(total(gram, others), "row", stages[0])
    lower_gram = passed_along(own_gram, "tm", 1)
    leaf = call(
        leaf_kernel,
        "leaf_roots",
        [
            shape(2 * n, n),
            shape(2, 2 * n, 4 * n, kind=BF16),
            shape(2, 2 * n, 2 * n, kind=BF16),
            shape(2, 2, 2 * n, 2 * n, kind=BF16),
        ],
        in_specs=[IN_VMEM] * 3,
        out_specs=[IN_VMEM] * 4,
    )(lower_gram, own_gram, sketch)
    for bits in stages[:0:-1]:
        beside = leaf if bits == stages[1] else own_gram
        others, beside = lax.optimization_barrier((received(mine, "row", bits), beside))
        mine = total(mine, others)
        if bits == stages[1]:
            leaf = beside
    (theirs,) = received(mine, "row", stages[0])
    chunks = 4
    return tuple(
        call(
            merge_kernel,
            "merge",
            [shape(n, n), shape(rows, n)],
            in_specs=[IN_VMEM] * 10,
            out_specs=[ANYWHERE, ANYWHERE],
            scratch_shapes=[
                pltpu.VMEM((n, n), F32),
                pltpu.VMEM((rows, n), F32),
                pltpu.SemaphoreType.DMA,
                pltpu.SemaphoreType.DMA((chunks,)),
            ],
        )(mine, theirs, *leaf, *parts, snapshots)
    )


def product_t(left, right):
    return jnp.dot(left.T, right, precision=HIGHEST, preferred_element_type=F32)


def product(left, right):
    return jnp.dot(left, right, precision=HIGHEST, preferred_element_type=F32)


def inverse_root(matrix):
    frob_scale = jnp.sqrt(jnp.sum(matrix * matrix) + 1e-06)
    ident = jnp.eye(matrix.shape[0], dtype=matrix.dtype)
    y_iter = matrix / frob_scale
    z_iter = ident
    for repeat in range(NS_STEPS):
        middle = 1.5 * ident - 0.5 * product(z_iter, y_iter)
        y_iter = product(y_iter, middle)
        z_iter = product(middle, z_iter)
    return z_iter / jnp.sqrt(frob_scale)


def many_merges(snapshots, sketches, tree_depth):
    leaf_sum = row_sum(product_t(snapshots, snapshots))
    leaf_root = inverse_root(leaf_sum)
    mode_block = product(snapshots, leaf_root)
    own_gram = product_t(leaf_root, product(leaf_sum, leaf_root))
    for tree_level in range(tree_depth):
        sketch = sketches[tree_level]
        lower_block, lower_gram = passed_along((mode_block, own_gram), "tm", 1 << tree_level)
        cross_sum = row_sum(product_t(lower_block, mode_block))
        top_rows = jnp.concatenate([lower_gram, cross_sum], axis=1)
        bottom_rows = jnp.concatenate([cross_sum.T, own_gram], axis=1)
        gram_sum = jnp.concatenate([top_rows, bottom_rows], axis=0)
        joined = jnp.concatenate([lower_block, mode_block], axis=1)
        reduced = product(gram_sum, sketch)
        small = product_t(reduced, product(gram_sum, reduced))
        mixing = product(reduced, inverse_root(small))
        mode_block = product(joined, mixing)
        own_gram = product_t(mixing, product(gram_sum, mixing))
    coefficients = row_sum(product_t(mode_block, snapshots))
    deflated = snapshots - product(mode_block, coefficients)
    return coefficients, deflated


def body(snapshots, sketches):
    tree_depth = lax.axis_size("tm").bit_length() - 1
    if tree_depth == 1:
        return one_merge(snapshots, sketches[0])
    return many_merges(snapshots, sketches, tree_depth)


def solution(mesh):
    placed = (P("row", "tm"), P())
    return jax.shard_map(
        body, mesh=mesh, in_specs=placed, out_specs=(P(None, "tm"), P("row", "tm")), check_vma=False
    )
```

```python
import jax
import jax.numpy as jnp
from jax import lax
from jax.experimental import pallas as pl
from jax.experimental.pallas import tpu as pltpu
from jax.sharding import PartitionSpec as P

NS_STEPS = 5
HIGHEST = lax.Precision.HIGHEST
F32 = jnp.float32
BF16 = jnp.bfloat16
IN_VMEM = pl.BlockSpec(memory_space=pltpu.VMEM)
LIMITED = pltpu.CompilerParams(vmem_limit_bytes=12 << 20)
ANYWHERE = pl.BlockSpec(memory_space=pl.ANY)


def split(x):
    high = x.astype(BF16)
    rest = x - high.astype(F32)
    middle = rest.astype(BF16)
    low = (rest - middle.astype(F32)).astype(BF16)
    return high, middle, low


def dot(left, right):
    return jnp.dot(left, right, preferred_element_type=F32)


def dot_t(left, right):
    return lax.dot_general(left, right, (((0,), (0,)), ((), ())), preferred_element_type=F32)


def dot_nt(left, right):
    return lax.dot_general(left, right, (((1,), (1,)), ((), ())), preferred_element_type=F32)


def mul(left, right):
    lh, lm, ll = left
    rh, rm, rl = right
    n = rh.shape[1]
    both = jnp.concatenate([jnp.concatenate([rh, rm], 1), jnp.concatenate([rm, rh], 1)], 0)
    wide = dot(jnp.concatenate([lh, lm], 1), both)
    small = dot(jnp.concatenate([ll, lh], 1), jnp.concatenate([rh, rl], 0))
    return wide[:, :n] + (wide[:, n:] + small)


def mul_t(left, right):
    lh, lm, ll = left
    rh, rm, rl = right
    k, n = lh.shape[1], rh.shape[1]
    wide = dot_t(jnp.concatenate([lh, lm, ll], 1), jnp.concatenate([rh, rm], 1))
    small = dot_t(lh, rl)
    return wide[:k, :n] + ((wide[:k, n:] + wide[k : 2 * k, :n]) + (wide[k : 2 * k, n:] + (wide[2 * k :, :n] + small)))


def mul_nt(left, right):
    k, n = left[0].shape[0], right[0].shape[0]
    wide = dot_nt(jnp.concatenate(left, 0), jnp.concatenate(right[:2], 0))
    small = dot_nt(left[0], right[2])
    return wide[:k, :n] + ((wide[:k, n:] + wide[k : 2 * k, :n]) + (wide[k : 2 * k, n:] + (wide[2 * k :, :n] + small)))


def identity(size):
    return (
        lax.broadcasted_iota(jnp.int32, (size, size), 0) == lax.broadcasted_iota(jnp.int32, (size, size), 1)
    ).astype(F32)


def root_iteration(matrices, beside=lambda step: None):
    eye = identity(matrices[0].shape[0])
    squares = []
    for a in matrices:
        parts = split(a)
        squares.append(mul(parts, parts))
    beside(0)
    scales = [jnp.sqrt(jnp.sum(a * a, keepdims=True) + 1e-06) for a in matrices]
    ys, zs = [], []
    for a, square, scale in zip(matrices, squares, scales):
        inverse = 1.0 / scale
        y = a * inverse
        ys.append(1.5 * y - (0.5 * inverse * inverse) * square)
        zs.append(1.5 * eye - 0.5 * y)
    for repeat in range(1, NS_STEPS):
        y_parts, z_parts = [split(y) for y in ys], [split(z) for z in zs]
        middles = [1.5 * eye - 0.5 * mul(z, y) for z, y in zip(z_parts, y_parts)]
        if repeat == NS_STEPS - 1:
            return zs, middles, scales
        beside(2 * repeat - 1)
        m_parts = [split(m) for m in middles]
        ys = [mul(y, m) for y, m in zip(y_parts, m_parts)]
        zs = [mul(m, z) for z, m in zip(z_parts, m_parts)]
        beside(2 * repeat)


def gram_kernel(x_ref, out_ref):
    k = x_ref.shape[1]
    h, m, l = split(x_ref[...])
    wide = dot_t(jnp.concatenate([h, m, l], 1), jnp.concatenate([h, m], 1))
    cross = wide[:k, k:] + wide[2 * k :, :k]
    out_ref[...] = (wide[:k, :k] + wide[k : 2 * k, k:]) + (cross + cross.T)


def upper_half():
    return lax.rem(lax.axis_index("row"), 2) == 1


def cross_kernel(left_ref, right_ref, mine_ref, theirs_ref):
    gram = mul_t(split(left_ref[...]), split(right_ref[...]))
    half = gram.shape[0] // 2
    upper = upper_half()
    mine_ref[...] = jnp.where(upper, gram[half:], gram[:half])
    theirs_ref[...] = jnp.where(upper, gram[:half], gram[half:])


def packed(parts):
    high, middle, low = parts
    return jnp.concatenate([high, middle], 1), jnp.concatenate([low, high], 1)


def weights(parts):
    high, middle, low = parts
    both = jnp.concatenate([jnp.concatenate([high, middle], 1), jnp.concatenate([middle, high], 1)], 0)
    return both, jnp.concatenate([high, low], 0)


def mul_packed(left, right):
    n = right[1].shape[1]
    wide = dot(left[0], right[0])
    return wide[:, :n] + (wide[:, n:] + dot(left[1], right[1]))


def split_kernel(lower_ref, own_ref, high_ref, middle_ref, low_ref):
    n = own_ref.shape[1]
    for at, ref in enumerate((lower_ref, own_ref)):
        columns = slice(at * n, (at + 1) * n)
        high_ref[:, columns], middle_ref[:, columns], low_ref[:, columns] = split(ref[...])


def leaf_kernel(lower_ref, own_ref, sketch_ref, f_ref, left_ref, wide_ref, small_ref):
    n = own_ref.shape[0]
    grams = [lower_ref[...], own_ref[...]]
    zs, middles, scales = root_iteration(grams)
    roots = [mul(split(m), split(z)) * lax.rsqrt(c) for z, m, c in zip(zs, middles, scales)]
    for at, (gram, root) in enumerate(zip(grams, roots)):
        root_parts, gram_parts = split(root), split(gram)
        e = mul(root_parts, split(sketch_ref[at * n : (at + 1) * n, :]))
        m = mul(root_parts, split(root.T))
        lefts = packed(split(jnp.concatenate([e.T, m], 0)))
        products = mul_packed(lefts, weights(gram_parts))
        f_ref[at] = products[:n]
        left_ref[at, 0], left_ref[at, 1] = lefts
        wide_ref[at], small_ref[at] = weights(split(jnp.concatenate([m, products[n:]], 1)))


def merge_kernel(
    mine_ref, theirs_ref, f_ref, left_ref, wide_ref, small_ref, high_ref, middle_ref, low_ref, own_ref,
    coef_ref, out_ref, coef_stage_ref, stage_ref, wide_modes_ref, small_modes_ref, coef_sem, sems,
):
    n = mine_ref.shape[1]
    upper = upper_half()
    mine, theirs = mine_ref[...], theirs_ref[...]
    cross = jnp.concatenate([jnp.where(upper, theirs, mine), jnp.where(upper, mine, theirs)], 0)
    from_lower = mul_packed((left_ref[0, 0], left_ref[0, 1]), weights(split(cross)))
    from_own = mul_packed((left_ref[1, 0], left_ref[1, 1]), weights(split(cross.T)))
    lower_f, own_f = split(f_ref[0] + from_own[:n]), split(f_ref[1] + from_lower[:n])
    lower = mul_packed(packed(lower_f), (wide_ref[0], small_ref[0]))
    own = mul_packed(packed(own_f), (wide_ref[1], small_ref[1]))
    lower_p = lower[:, n:] + mul(own_f, split(from_own[n:]))
    own_p = own[:, n:] + mul(lower_f, split(from_lower[n:]))
    v = jnp.concatenate([lower[:, :n], own[:, :n]], 1)
    p = jnp.concatenate([lower_p, own_p], 1)
    rows, chunks = own_ref.shape[0], sems.shape[0]
    step = rows // chunks
    slices = [slice(at * step, (at + 1) * step) for at in range(chunks)]
    v_high, v_middle, v_low = split(v.T)
    v_both = jnp.concatenate([v_high, v_middle], 1)
    pieces = 4

    def one_piece(at):
        if at >= pieces:
            return
        here = slice(at * rows // pieces, (at + 1) * rows // pieces)
        high = high_ref[here, :]
        first, second = dot(high, v_both), dot(middle_ref[here, :], v_both)
        third = dot(low_ref[here, :], v_high) + dot(high, v_low)
        modes = first[:, :n] + ((first[:, n:] + second[:, :n]) + (second[:, n:] + third))
        wide_modes_ref[here, :], small_modes_ref[here, :] = packed(split(modes))

    (z,), (middle,), (scale,) = root_iteration([mul_nt(split(v), split(p))], one_piece)
    z_parts, middle_parts = split(z), split(middle)
    zp = split(mul(z_parts, split(own_p)))
    coefficients = mul(middle_parts, zp) * lax.rsqrt(scale)
    coef_stage_ref[...] = coefficients
    coef_copy = pltpu.make_async_copy(coef_stage_ref, coef_ref, coef_sem)
    coef_copy.start()
    mixed = mul(split(mul(middle_parts, middle_parts)), split(mul(z_parts, zp))) / scale
    mixed_wide, mixed_small = weights(split(mixed))
    copies = []
    for at, here in enumerate(slices):
        wide = dot(wide_modes_ref[here, :], mixed_wide)
        small = dot(small_modes_ref[here, :], mixed_small)
        stage_ref[here, :] = own_ref[here, :] - (wide[:, :n] + (wide[:, n:] + small))
        copy = pltpu.make_async_copy(stage_ref.at[here], out_ref.at[here], sems.at[at])
        copy.start()
        copies.append(copy)
    for copy in copies:
        copy.wait()
    coef_copy.wait()


def shape(*dims, kind=F32):
    return jax.ShapeDtypeStruct(dims, kind)


def passed_along(block, axis, distance):
    devices = range(lax.axis_size(axis))
    route = [((i - distance) % len(devices), i) for i in devices]
    return lax.ppermute(block, axis, route)


def stages_of(size):
    bits = [1 << b for b in range(size.bit_length() - 1)]
    stages, rest = [(b,) for b in bits[:1]], bits[1:]
    while rest:
        stages.append(tuple(rest[:2]))
        rest = rest[2:]
    return stages


def received(part, axis, bits):
    flips = [bits[0]] if len(bits) == 1 else [bits[0], bits[1], bits[0] | bits[1]]
    size = lax.axis_size(axis)
    return [lax.ppermute(part, axis, [(i, i ^ flip) for i in range(size)]) for flip in flips]


def total(part, others):
    if len(others) == 1:
        return part + others[0]
    return (part + others[0]) + (others[1] + others[2])


def summed_over(part, axis, bits):
    return total(part, received(part, axis, bits))


def row_sum(part, axis="row"):
    size = lax.axis_size(axis)
    if size & (size - 1):
        return lax.psum(part, axis)
    for bits in stages_of(size):
        part = summed_over(part, axis, bits)
    return part


def call(kernel, name, outs, **more):
    return pl.pallas_call(kernel, out_shape=outs, compiler_params=LIMITED, name=name, **more)


def one_merge(snapshots, sketch):
    rows, n = snapshots.shape
    lower = passed_along(snapshots, "tm", 1)
    stages = stages_of(lax.axis_size("row"))
    gram = call(gram_kernel, "own_gram", shape(n, n), in_specs=[IN_VMEM], out_specs=IN_VMEM)(snapshots)
    for bits in stages[1:-1]:
        gram = summed_over(gram, "row", bits)
    mine, theirs = call(
        cross_kernel, "cross_gram", [shape(n // 2, n)] * 2, in_specs=[IN_VMEM] * 2, out_specs=[IN_VMEM] * 2
    )(lower, snapshots)
    parts = call(
        split_kernel, "raw_parts", [shape(rows, 2 * n, kind=BF16)] * 3, in_specs=[IN_VMEM] * 2, out_specs=[IN_VMEM] * 3
    )(lower, snapshots)
    others = received(theirs, "row", stages[0])
    others, parts = lax.optimization_barrier((others, parts))
    mine = total(mine, others)
    others, _ = lax.optimization_barrier((received(gram, "row", stages[-1]), mine))
    own_gram = summed_over(total(gram, others), "row", stages[0])
    lower_gram = passed_along(own_gram, "tm", 1)
    leaf = call(
        leaf_kernel,
        "leaf_roots",
        [
            shape(2, n, n),
            shape(2, 2, 2 * n, 2 * n, kind=BF16),
            shape(2, 2 * n, 4 * n, kind=BF16),
            shape(2, 2 * n, 2 * n, kind=BF16),
        ],
        in_specs=[IN_VMEM] * 3,
        out_specs=[IN_VMEM] * 4,
    )(lower_gram, own_gram, sketch)
    for bits in stages[:0:-1]:
        beside = leaf if bits == stages[1] else own_gram
        others, beside = lax.optimization_barrier((received(mine, "row", bits), beside))
        mine = total(mine, others)
        if bits == stages[1]:
            leaf = beside
    (theirs,) = received(mine, "row", stages[0])
    chunks = 4
    return tuple(
        call(
            merge_kernel,
            "merge",
            [shape(n, n), shape(rows, n)],
            in_specs=[IN_VMEM] * 10,
            out_specs=[ANYWHERE, ANYWHERE],
            scratch_shapes=[
                pltpu.VMEM((n, n), F32),
                pltpu.VMEM((rows, n), F32),
                pltpu.VMEM((rows, 2 * n), BF16),
                pltpu.VMEM((rows, 2 * n), BF16),
                pltpu.SemaphoreType.DMA,
                pltpu.SemaphoreType.DMA((chunks,)),
            ],
        )(mine, theirs, *leaf, *parts, snapshots)
    )


def product_t(left, right):
    return jnp.dot(left.T, right, precision=HIGHEST, preferred_element_type=F32)


def product(left, right):
    return jnp.dot(left, right, precision=HIGHEST, preferred_element_type=F32)


def inverse_root(matrix):
    frob_scale = jnp.sqrt(jnp.sum(matrix * matrix) + 1e-06)
    ident = jnp.eye(matrix.shape[0], dtype=matrix.dtype)
    y_iter = matrix / frob_scale
    z_iter = ident
    for repeat in range(NS_STEPS):
        middle = 1.5 * ident - 0.5 * product(z_iter, y_iter)
        y_iter = product(y_iter, middle)
        z_iter = product(middle, z_iter)
    return z_iter / jnp.sqrt(frob_scale)


def many_merges(snapshots, sketches, tree_depth):
    leaf_sum = row_sum(product_t(snapshots, snapshots))
    leaf_root = inverse_root(leaf_sum)
    mode_block = product(snapshots, leaf_root)
    own_gram = product_t(leaf_root, product(leaf_sum, leaf_root))
    for tree_level in range(tree_depth):
        sketch = sketches[tree_level]
        lower_block, lower_gram = passed_along((mode_block, own_gram), "tm", 1 << tree_level)
        cross_sum = row_sum(product_t(lower_block, mode_block))
        top_rows = jnp.concatenate([lower_gram, cross_sum], axis=1)
        bottom_rows = jnp.concatenate([cross_sum.T, own_gram], axis=1)
        gram_sum = jnp.concatenate([top_rows, bottom_rows], axis=0)
        joined = jnp.concatenate([lower_block, mode_block], axis=1)
        reduced = product(gram_sum, sketch)
        small = product_t(reduced, product(gram_sum, reduced))
        mixing = product(reduced, inverse_root(small))
        mode_block = product(joined, mixing)
        own_gram = product_t(mixing, product(gram_sum, mixing))
    coefficients = row_sum(product_t(mode_block, snapshots))
    deflated = snapshots - product(mode_block, coefficients)
    return coefficients, deflated


def body(snapshots, sketches):
    tree_depth = lax.axis_size("tm").bit_length() - 1
    row_count = lax.axis_size("row")
    if tree_depth == 1 and row_count >= 4 and row_count & (row_count - 1) == 0:
        return one_merge(snapshots, sketches[0])
    return many_merges(snapshots, sketches, tree_depth)


def solution(mesh):
    placed = (P("row", "tm"), P())
    return jax.shard_map(
        body, mesh=mesh, in_specs=placed, out_specs=(P(None, "tm"), P("row", "tm")), check_vma=False
    )
```

```python
import jax
import jax.numpy as jnp
from jax import lax
from jax.experimental import pallas as pl
from jax.experimental.pallas import tpu as pltpu
from jax.sharding import PartitionSpec as P

NS_STEPS = 5
HIGHEST = lax.Precision.HIGHEST
F32 = jnp.float32
BF16 = jnp.bfloat16
IN_VMEM = pl.BlockSpec(memory_space=pltpu.VMEM)
LIMITED = pltpu.CompilerParams(vmem_limit_bytes=12 << 20)
ANYWHERE = pl.BlockSpec(memory_space=pl.ANY)


def split(x):
    high = x.astype(BF16)
    rest = x - high.astype(F32)
    middle = rest.astype(BF16)
    low = (rest - middle.astype(F32)).astype(BF16)
    return high, middle, low


def dot(left, right):
    return jnp.dot(left, right, preferred_element_type=F32)


def dot_t(left, right):
    return lax.dot_general(left, right, (((0,), (0,)), ((), ())), preferred_element_type=F32)


def dot_nt(left, right):
    return lax.dot_general(left, right, (((1,), (1,)), ((), ())), preferred_element_type=F32)


def mul(left, right):
    lh, lm, ll = left
    rh, rm, rl = right
    n = rh.shape[1]
    both = jnp.concatenate([jnp.concatenate([rh, rm], 1), jnp.concatenate([rm, rh], 1)], 0)
    small = dot(jnp.concatenate([ll, lh], 1), jnp.concatenate([rh, rl], 0))
    wide = dot(jnp.concatenate([lh, lm], 1), both)
    return wide[:, :n] + (wide[:, n:] + small)


def mul_t(left, right):
    lh, lm, ll = left
    rh, rm, rl = right
    k, n = lh.shape[1], rh.shape[1]
    wide = dot_t(jnp.concatenate([lh, lm, ll], 1), jnp.concatenate([rh, rm], 1))
    small = dot_t(lh, rl)
    return wide[:k, :n] + ((wide[:k, n:] + wide[k : 2 * k, :n]) + (wide[k : 2 * k, n:] + (wide[2 * k :, :n] + small)))


def mul_nt(left, right):
    k, n = left[0].shape[0], right[0].shape[0]
    wide = dot_nt(jnp.concatenate(left, 0), jnp.concatenate(right[:2], 0))
    small = dot_nt(left[0], right[2])
    return wide[:k, :n] + ((wide[:k, n:] + wide[k : 2 * k, :n]) + (wide[k : 2 * k, n:] + (wide[2 * k :, :n] + small)))


def identity(size):
    return (
        lax.broadcasted_iota(jnp.int32, (size, size), 0) == lax.broadcasted_iota(jnp.int32, (size, size), 1)
    ).astype(F32)


def root_iteration(matrices, beside=lambda step: None):
    eye = identity(matrices[0].shape[0])
    squares = []
    for a in matrices:
        parts = split(a)
        squares.append(mul(parts, parts))
    beside(0)
    scales = [jnp.sqrt(jnp.sum(a * a, keepdims=True) + 1e-06) for a in matrices]
    ys, zs = [], []
    for a, square, scale in zip(matrices, squares, scales):
        inverse = 1.0 / scale
        y = a * inverse
        ys.append(1.5 * y - (0.5 * inverse * inverse) * square)
        zs.append(1.5 * eye - 0.5 * y)
    for repeat in range(1, NS_STEPS):
        y_parts, z_parts = [split(y) for y in ys], [split(z) for z in zs]
        middles = [1.5 * eye - 0.5 * mul(z, y) for z, y in zip(z_parts, y_parts)]
        if repeat == NS_STEPS - 1:
            return zs, middles, scales
        beside(2 * repeat - 1)
        m_parts = [split(m) for m in middles]
        ys = [mul(y, m) for y, m in zip(y_parts, m_parts)]
        zs = [mul(m, z) for z, m in zip(z_parts, m_parts)]
        beside(2 * repeat)


def gram_kernel(x_ref, out_ref):
    k = x_ref.shape[1]
    h, m, l = split(x_ref[...])
    wide = dot_t(jnp.concatenate([h, m, l], 1), jnp.concatenate([h, m], 1))
    cross = wide[:k, k:] + wide[2 * k :, :k]
    out_ref[...] = (wide[:k, :k] + wide[k : 2 * k, k:]) + (cross + cross.T)


def upper_half():
    return lax.rem(lax.axis_index("row"), 2) == 1


def cross_kernel(left_ref, right_ref, mine_ref, theirs_ref):
    gram = mul_t(split(left_ref[...]), split(right_ref[...]))
    half = gram.shape[0] // 2
    upper = upper_half()
    mine_ref[...] = jnp.where(upper, gram[half:], gram[:half])
    theirs_ref[...] = jnp.where(upper, gram[:half], gram[half:])


def packed(parts):
    high, middle, low = parts
    return jnp.concatenate([high, middle], 1), jnp.concatenate([low, high], 1)


def weights(parts):
    high, middle, low = parts
    both = jnp.concatenate([jnp.concatenate([high, middle], 1), jnp.concatenate([middle, high], 1)], 0)
    return both, jnp.concatenate([high, low], 0)


def mul_packed(left, right):
    n = right[1].shape[1]
    wide = dot(left[0], right[0])
    return wide[:, :n] + (wide[:, n:] + dot(left[1], right[1]))


def split_kernel(lower_ref, own_ref, high_ref, middle_ref, low_ref):
    n = own_ref.shape[1]
    for at, ref in enumerate((lower_ref, own_ref)):
        columns = slice(at * n, (at + 1) * n)
        high_ref[:, columns], middle_ref[:, columns], low_ref[:, columns] = split(ref[...])


def leaf_kernel(lower_ref, own_ref, sketch_ref, f_ref, left_ref, wide_ref, small_ref):
    n = own_ref.shape[0]
    grams = [lower_ref[...], own_ref[...]]
    zs, middles, scales = root_iteration(grams)
    roots = [mul(split(m), split(z)) * lax.rsqrt(c) for z, m, c in zip(zs, middles, scales)]
    for at, (gram, root) in enumerate(zip(grams, roots)):
        root_parts, gram_parts = split(root), split(gram)
        e = mul(root_parts, split(sketch_ref[at * n : (at + 1) * n, :]))
        m = mul(root_parts, split(root.T))
        lefts = packed(split(jnp.concatenate([e.T, m], 0)))
        products = mul_packed(lefts, weights(gram_parts))
        f_ref[at] = products[:n]
        left_ref[at, 0], left_ref[at, 1] = lefts
        wide_ref[at], small_ref[at] = weights(split(jnp.concatenate([m, products[n:]], 1)))


def merge_kernel(
    mine_ref, theirs_ref, f_ref, left_ref, wide_ref, small_ref, high_ref, middle_ref, low_ref, own_ref,
    coef_ref, out_ref, coef_stage_ref, stage_ref, wide_modes_ref, small_modes_ref, coef_sem, sems,
):
    n = mine_ref.shape[1]
    upper = upper_half()
    mine, theirs = mine_ref[...], theirs_ref[...]
    cross = jnp.concatenate([jnp.where(upper, theirs, mine), jnp.where(upper, mine, theirs)], 0)
    from_lower = mul_packed((left_ref[0, 0], left_ref[0, 1]), weights(split(cross)))
    from_own = mul_packed((left_ref[1, 0], left_ref[1, 1]), weights(split(cross.T)))
    lower_f, own_f = split(f_ref[0] + from_own[:n]), split(f_ref[1] + from_lower[:n])
    lower = mul_packed(packed(lower_f), (wide_ref[0], small_ref[0]))
    own = mul_packed(packed(own_f), (wide_ref[1], small_ref[1]))
    lower_p = lower[:, n:] + mul(own_f, split(from_own[n:]))
    own_p = own[:, n:] + mul(lower_f, split(from_lower[n:]))
    v = jnp.concatenate([lower[:, :n], own[:, :n]], 1)
    p = jnp.concatenate([lower_p, own_p], 1)
    rows, chunks = own_ref.shape[0], sems.shape[0]
    step = rows // chunks
    slices = [slice(at * step, (at + 1) * step) for at in range(chunks)]
    v_high, v_middle, v_low = split(v.T)
    v_both = jnp.concatenate([v_high, v_middle], 1)
    pieces = 4

    def one_piece(at):
        if at >= pieces:
            return
        here = slice(at * rows // pieces, (at + 1) * rows // pieces)
        high = high_ref[here, :]
        first, second = dot(high, v_both), dot(middle_ref[here, :], v_both)
        third = dot(low_ref[here, :], v_high) + dot(high, v_low)
        modes = first[:, :n] + ((first[:, n:] + second[:, :n]) + (second[:, n:] + third))
        wide_modes_ref[here, :], small_modes_ref[here, :] = packed(split(modes))

    (z,), (middle,), (scale,) = root_iteration([mul_nt(split(v), split(p))], one_piece)
    z_parts, middle_parts = split(z), split(middle)
    zp = split(mul(z_parts, split(own_p)))
    coefficients = mul(middle_parts, zp) * lax.rsqrt(scale)
    coef_stage_ref[...] = coefficients
    coef_copy = pltpu.make_async_copy(coef_stage_ref, coef_ref, coef_sem)
    coef_copy.start()
    mixed = mul(split(mul(middle_parts, middle_parts)), split(mul(z_parts, zp))) / scale
    mixed_wide, mixed_small = weights(split(mixed))
    copies = []
    for at, here in enumerate(slices):
        wide = dot(wide_modes_ref[here, :], mixed_wide)
        small = dot(small_modes_ref[here, :], mixed_small)
        stage_ref[here, :] = own_ref[here, :] - (wide[:, :n] + (wide[:, n:] + small))
        copy = pltpu.make_async_copy(stage_ref.at[here], out_ref.at[here], sems.at[at])
        copy.start()
        copies.append(copy)
    for copy in copies:
        copy.wait()
    coef_copy.wait()


def shape(*dims, kind=F32):
    return jax.ShapeDtypeStruct(dims, kind)


def passed_along(block, axis, distance):
    devices = range(lax.axis_size(axis))
    route = [((i - distance) % len(devices), i) for i in devices]
    return lax.ppermute(block, axis, route)


def stages_of(size):
    bits = [1 << b for b in range(size.bit_length() - 1)]
    stages, rest = [(b,) for b in bits[:1]], bits[1:]
    while rest:
        stages.append(tuple(rest[:2]))
        rest = rest[2:]
    return stages


def received(part, axis, bits):
    flips = [bits[0]] if len(bits) == 1 else [bits[0], bits[1], bits[0] | bits[1]]
    size = lax.axis_size(axis)
    return [lax.ppermute(part, axis, [(i, i ^ flip) for i in range(size)]) for flip in flips]


def total(part, others):
    if len(others) == 1:
        return part + others[0]
    return (part + others[0]) + (others[1] + others[2])


def summed_over(part, axis, bits):
    return total(part, received(part, axis, bits))


def row_sum(part, axis="row"):
    size = lax.axis_size(axis)
    if size & (size - 1):
        return lax.psum(part, axis)
    for bits in stages_of(size):
        part = summed_over(part, axis, bits)
    return part


def call(kernel, name, outs, **more):
    return pl.pallas_call(kernel, out_shape=outs, compiler_params=LIMITED, name=name, **more)


def one_merge(snapshots, sketch):
    rows, n = snapshots.shape
    lower = passed_along(snapshots, "tm", 1)
    stages = stages_of(lax.axis_size("row"))
    gram = call(gram_kernel, "own_gram", shape(n, n), in_specs=[IN_VMEM], out_specs=IN_VMEM)(snapshots)
    for bits in stages[1:-1]:
        gram = summed_over(gram, "row", bits)
    mine, theirs = call(
        cross_kernel, "cross_gram", [shape(n // 2, n)] * 2, in_specs=[IN_VMEM] * 2, out_specs=[IN_VMEM] * 2
    )(lower, snapshots)
    parts = call(
        split_kernel, "raw_parts", [shape(rows, 2 * n, kind=BF16)] * 3, in_specs=[IN_VMEM] * 2, out_specs=[IN_VMEM] * 3
    )(lower, snapshots)
    others = received(theirs, "row", stages[0])
    others, parts = lax.optimization_barrier((others, parts))
    mine = total(mine, others)
    others, _ = lax.optimization_barrier((received(gram, "row", stages[-1]), mine))
    own_gram = summed_over(total(gram, others), "row", stages[0])
    lower_gram = passed_along(own_gram, "tm", 1)
    leaf = call(
        leaf_kernel,
        "leaf_roots",
        [
            shape(2, n, n),
            shape(2, 2, 2 * n, 2 * n, kind=BF16),
            shape(2, 2 * n, 4 * n, kind=BF16),
            shape(2, 2 * n, 2 * n, kind=BF16),
        ],
        in_specs=[IN_VMEM] * 3,
        out_specs=[IN_VMEM] * 4,
    )(lower_gram, own_gram, sketch)
    for bits in stages[:0:-1]:
        beside = leaf if bits == stages[1] else own_gram
        others, beside = lax.optimization_barrier((received(mine, "row", bits), beside))
        mine = total(mine, others)
        if bits == stages[1]:
            leaf = beside
    (theirs,) = received(mine, "row", stages[0])
    chunks = 4
    return tuple(
        call(
            merge_kernel,
            "merge",
            [shape(n, n), shape(rows, n)],
            in_specs=[IN_VMEM] * 10,
            out_specs=[ANYWHERE, ANYWHERE],
            scratch_shapes=[
                pltpu.VMEM((n, n), F32),
                pltpu.VMEM((rows, n), F32),
                pltpu.VMEM((rows, 2 * n), BF16),
                pltpu.VMEM((rows, 2 * n), BF16),
                pltpu.SemaphoreType.DMA,
                pltpu.SemaphoreType.DMA((chunks,)),
            ],
        )(mine, theirs, *leaf, *parts, snapshots)
    )


def product_t(left, right):
    return jnp.dot(left.T, right, precision=HIGHEST, preferred_element_type=F32)


def product(left, right):
    return jnp.dot(left, right, precision=HIGHEST, preferred_element_type=F32)


def inverse_root(matrix):
    frob_scale = jnp.sqrt(jnp.sum(matrix * matrix) + 1e-06)
    ident = jnp.eye(matrix.shape[0], dtype=matrix.dtype)
    y_iter = matrix / frob_scale
    z_iter = ident
    for repeat in range(NS_STEPS):
        middle = 1.5 * ident - 0.5 * product(z_iter, y_iter)
        y_iter = product(y_iter, middle)
        z_iter = product(middle, z_iter)
    return z_iter / jnp.sqrt(frob_scale)


def many_merges(snapshots, sketches, tree_depth):
    leaf_sum = row_sum(product_t(snapshots, snapshots))
    leaf_root = inverse_root(leaf_sum)
    mode_block = product(snapshots, leaf_root)
    own_gram = product_t(leaf_root, product(leaf_sum, leaf_root))
    for tree_level in range(tree_depth):
        sketch = sketches[tree_level]
        lower_block, lower_gram = passed_along((mode_block, own_gram), "tm", 1 << tree_level)
        cross_sum = row_sum(product_t(lower_block, mode_block))
        top_rows = jnp.concatenate([lower_gram, cross_sum], axis=1)
        bottom_rows = jnp.concatenate([cross_sum.T, own_gram], axis=1)
        gram_sum = jnp.concatenate([top_rows, bottom_rows], axis=0)
        joined = jnp.concatenate([lower_block, mode_block], axis=1)
        reduced = product(gram_sum, sketch)
        small = product_t(reduced, product(gram_sum, reduced))
        mixing = product(reduced, inverse_root(small))
        mode_block = product(joined, mixing)
        own_gram = product_t(mixing, product(gram_sum, mixing))
    coefficients = row_sum(product_t(mode_block, snapshots))
    deflated = snapshots - product(mode_block, coefficients)
    return coefficients, deflated


def body(snapshots, sketches):
    tree_depth = lax.axis_size("tm").bit_length() - 1
    row_count = lax.axis_size("row")
    if tree_depth == 1 and row_count >= 4 and row_count & (row_count - 1) == 0:
        return one_merge(snapshots, sketches[0])
    return many_merges(snapshots, sketches, tree_depth)


def solution(mesh):
    placed = (P("row", "tm"), P())
    return jax.shard_map(
        body, mesh=mesh, in_specs=placed, out_specs=(P(None, "tm"), P("row", "tm")), check_vma=False
    )
```

```python
import jax
import jax.numpy as jnp
from jax import lax
from jax.experimental import pallas as pl
from jax.experimental.pallas import tpu as pltpu
from jax.sharding import PartitionSpec as P

NS_STEPS = 5
HIGHEST = lax.Precision.HIGHEST
F32 = jnp.float32
BF16 = jnp.bfloat16
IN_VMEM = pl.BlockSpec(memory_space=pltpu.VMEM)
LIMITED = pltpu.CompilerParams(vmem_limit_bytes=12 << 20)
ANYWHERE = pl.BlockSpec(memory_space=pl.ANY)


def split(x):
    high = x.astype(BF16)
    rest = x - high.astype(F32)
    middle = rest.astype(BF16)
    low = (rest - middle.astype(F32)).astype(BF16)
    return high, middle, low


def dot(left, right):
    return jnp.dot(left, right, preferred_element_type=F32)


def dot_t(left, right):
    return lax.dot_general(left, right, (((0,), (0,)), ((), ())), preferred_element_type=F32)


def dot_nt(left, right):
    return lax.dot_general(left, right, (((1,), (1,)), ((), ())), preferred_element_type=F32)


def mul(left, right):
    lh, lm, ll = left
    rh, rm, rl = right
    n = rh.shape[1]
    both = jnp.concatenate([jnp.concatenate([rh, rm], 1), jnp.concatenate([rm, rh], 1)], 0)
    wide = dot(jnp.concatenate([lh, lm], 1), both)
    small = dot(jnp.concatenate([ll, lh], 1), jnp.concatenate([rh, rl], 0))
    return wide[:, :n] + (wide[:, n:] + small)


def mul_t(left, right):
    lh, lm, ll = left
    rh, rm, rl = right
    k, n = lh.shape[1], rh.shape[1]
    wide = dot_t(jnp.concatenate([lh, lm, ll], 1), jnp.concatenate([rh, rm], 1))
    small = dot_t(lh, rl)
    return wide[:k, :n] + ((wide[:k, n:] + wide[k : 2 * k, :n]) + (wide[k : 2 * k, n:] + (wide[2 * k :, :n] + small)))


def mul_nt(left, right):
    k, n = left[0].shape[0], right[0].shape[0]
    wide = dot_nt(jnp.concatenate(left, 0), jnp.concatenate(right[:2], 0))
    small = dot_nt(left[0], right[2])
    return wide[:k, :n] + ((wide[:k, n:] + wide[k : 2 * k, :n]) + (wide[k : 2 * k, n:] + (wide[2 * k :, :n] + small)))


def identity(size):
    return (
        lax.broadcasted_iota(jnp.int32, (size, size), 0) == lax.broadcasted_iota(jnp.int32, (size, size), 1)
    ).astype(F32)


def root_iteration(matrices, beside=lambda step: None):
    eye = identity(matrices[0].shape[0])
    squares = []
    for a in matrices:
        parts = split(a)
        squares.append(mul(parts, parts))
    beside(0)
    scales = [jnp.sqrt(jnp.sum(a * a, keepdims=True) + 1e-06) for a in matrices]
    ys, zs = [], []
    for a, square, scale in zip(matrices, squares, scales):
        inverse = 1.0 / scale
        y = a * inverse
        ys.append(1.5 * y - (0.5 * inverse * inverse) * square)
        zs.append(1.5 * eye - 0.5 * y)
    for repeat in range(1, NS_STEPS):
        y_parts, z_parts = [split(y) for y in ys], [split(z) for z in zs]
        middles = [1.5 * eye - 0.5 * mul(z, y) for z, y in zip(z_parts, y_parts)]
        if repeat == NS_STEPS - 1:
            return zs, middles, scales
        beside(2 * repeat - 1)
        m_parts = [split(m) for m in middles]
        ys = [mul(y, m) for y, m in zip(y_parts, m_parts)]
        zs = [mul(m, z) for z, m in zip(z_parts, m_parts)]
        beside(2 * repeat)


def gram_kernel(x_ref, out_ref):
    k = x_ref.shape[1]
    h, m, l = split(x_ref[...])
    wide = dot_t(jnp.concatenate([h, m, l], 1), jnp.concatenate([h, m], 1))
    cross = wide[:k, k:] + wide[2 * k :, :k]
    out_ref[...] = (wide[:k, :k] + wide[k : 2 * k, k:]) + (cross + cross.T)


def upper_half():
    return lax.rem(lax.axis_index("row"), 2) == 1


def cross_kernel(left_ref, right_ref, mine_ref, theirs_ref):
    gram = mul_t(split(left_ref[...]), split(right_ref[...]))
    half = gram.shape[0] // 2
    upper = upper_half()
    mine_ref[...] = jnp.where(upper, gram[half:], gram[:half])
    theirs_ref[...] = jnp.where(upper, gram[:half], gram[half:])


def packed(parts):
    high, middle, low = parts
    return jnp.concatenate([high, middle], 1), jnp.concatenate([low, high], 1)


def weights(parts):
    high, middle, low = parts
    both = jnp.concatenate([jnp.concatenate([high, middle], 1), jnp.concatenate([middle, high], 1)], 0)
    return both, jnp.concatenate([high, low], 0)


def mul_packed(left, right):
    n = right[1].shape[1]
    wide = dot(left[0], right[0])
    return wide[:, :n] + (wide[:, n:] + dot(left[1], right[1]))


def split_kernel(lower_ref, own_ref, high_ref, middle_ref, low_ref):
    n = own_ref.shape[1]
    for at, ref in enumerate((lower_ref, own_ref)):
        columns = slice(at * n, (at + 1) * n)
        high_ref[:, columns], middle_ref[:, columns], low_ref[:, columns] = split(ref[...])


def leaf_kernel(lower_ref, own_ref, sketch_ref, f_ref, left_ref, wide_ref, small_ref):
    n = own_ref.shape[0]
    grams = [lower_ref[...], own_ref[...]]
    zs, middles, scales = root_iteration(grams)
    roots = [mul(split(m), split(z)) * lax.rsqrt(c) for z, m, c in zip(zs, middles, scales)]
    for at, (gram, root) in enumerate(zip(grams, roots)):
        root_parts, gram_parts = split(root), split(gram)
        e = mul(root_parts, split(sketch_ref[at * n : (at + 1) * n, :]))
        m = mul(root_parts, split(root.T))
        lefts = packed(split(jnp.concatenate([e.T, m], 0)))
        products = mul_packed(lefts, weights(gram_parts))
        f_ref[at] = products[:n]
        left_ref[at, 0], left_ref[at, 1] = lefts
        wide_ref[at], small_ref[at] = weights(split(jnp.concatenate([m, products[n:]], 1)))


def merge_kernel(
    mine_ref, theirs_ref, f_ref, left_ref, wide_ref, small_ref, high_ref, middle_ref, low_ref, own_ref,
    coef_ref, out_ref, coef_stage_ref, stage_ref, wide_modes_ref, small_modes_ref, coef_sem, sems,
):
    n = mine_ref.shape[1]
    upper = upper_half()
    mine, theirs = mine_ref[...], theirs_ref[...]
    cross = jnp.concatenate([jnp.where(upper, theirs, mine), jnp.where(upper, mine, theirs)], 0)
    from_lower = mul_packed((left_ref[0, 0], left_ref[0, 1]), weights(split(cross)))
    from_own = mul_packed((left_ref[1, 0], left_ref[1, 1]), weights(split(cross.T)))
    lower_f, own_f = split(f_ref[0] + from_own[:n]), split(f_ref[1] + from_lower[:n])
    lower = mul_packed(packed(lower_f), (wide_ref[0], small_ref[0]))
    own = mul_packed(packed(own_f), (wide_ref[1], small_ref[1]))
    lower_p = lower[:, n:] + mul(own_f, split(from_own[n:]))
    own_p = own[:, n:] + mul(lower_f, split(from_lower[n:]))
    v = jnp.concatenate([lower[:, :n], own[:, :n]], 1)
    p = jnp.concatenate([lower_p, own_p], 1)
    rows, chunks = own_ref.shape[0], sems.shape[0]
    step = rows // chunks
    slices = [slice(at * step, (at + 1) * step) for at in range(chunks)]
    v_high, v_middle, v_low = split(v.T)
    v_both = jnp.concatenate([v_high, v_middle], 1)
    pieces = 4

    def one_piece(at):
        if at >= pieces:
            return
        here = slice(at * rows // pieces, (at + 1) * rows // pieces)
        high = high_ref[here, :]
        first, second = dot(high, v_both), dot(middle_ref[here, :], v_both)
        third = dot(low_ref[here, :], v_high) + dot(high, v_low)
        modes = first[:, :n] + ((first[:, n:] + second[:, :n]) + (second[:, n:] + third))
        wide_modes_ref[here, :], small_modes_ref[here, :] = packed(split(modes))

    (z,), (middle,), (scale,) = root_iteration([mul_nt(split(v), split(p))], one_piece)
    z_parts, middle_parts = split(z), split(middle)
    zp = split(mul(z_parts, split(own_p)))
    coefficients = mul(middle_parts, zp) * lax.rsqrt(scale)
    coef_stage_ref[...] = coefficients
    coef_copy = pltpu.make_async_copy(coef_stage_ref, coef_ref, coef_sem)
    coef_copy.start()
    mixed = mul(split(mul(middle_parts, middle_parts)), split(mul(z_parts, zp))) / scale
    mixed_wide, mixed_small = weights(split(mixed))
    copies = []
    for at, here in enumerate(slices):
        wide = dot(wide_modes_ref[here, :], mixed_wide)
        small = dot(small_modes_ref[here, :], mixed_small)
        stage_ref[here, :] = own_ref[here, :] - (wide[:, :n] + (wide[:, n:] + small))
        copy = pltpu.make_async_copy(stage_ref.at[here], out_ref.at[here], sems.at[at])
        copy.start()
        copies.append(copy)
    for copy in copies:
        copy.wait()
    coef_copy.wait()


def shape(*dims, kind=F32):
    return jax.ShapeDtypeStruct(dims, kind)


def passed_along(block, axis, distance):
    devices = range(lax.axis_size(axis))
    route = [((i - distance) % len(devices), i) for i in devices]
    return lax.ppermute(block, axis, route)


def stages_of(size):
    bits = [1 << b for b in range(size.bit_length() - 1)]
    stages, rest = [(b,) for b in bits[:1]], bits[1:]
    while rest:
        stages.append(tuple(rest[:2]))
        rest = rest[2:]
    return stages


def received(part, axis, bits):
    flips = [bits[0]] if len(bits) == 1 else [bits[0], bits[1], bits[0] | bits[1]]
    size = lax.axis_size(axis)
    order = [2, 1, 0] if len(flips) == 3 else [0]
    moved = {at: lax.ppermute(part, axis, [(i, i ^ flips[at]) for i in range(size)]) for at in order}
    return [moved[at] for at in range(len(flips))]


def total(part, others):
    if len(others) == 1:
        return part + others[0]
    return (part + others[0]) + (others[1] + others[2])


def summed_over(part, axis, bits):
    return total(part, received(part, axis, bits))


def row_sum(part, axis="row"):
    size = lax.axis_size(axis)
    if size & (size - 1):
        return lax.psum(part, axis)
    for bits in stages_of(size):
        part = summed_over(part, axis, bits)
    return part


def call(kernel, name, outs, **more):
    return pl.pallas_call(kernel, out_shape=outs, compiler_params=LIMITED, name=name, **more)


def one_merge(snapshots, sketch):
    rows, n = snapshots.shape
    lower = passed_along(snapshots, "tm", 1)
    stages = stages_of(lax.axis_size("row"))
    gram = call(gram_kernel, "own_gram", shape(n, n), in_specs=[IN_VMEM], out_specs=IN_VMEM)(snapshots)
    for bits in stages[1:-1]:
        gram = summed_over(gram, "row", bits)
    mine, theirs = call(
        cross_kernel, "cross_gram", [shape(n // 2, n)] * 2, in_specs=[IN_VMEM] * 2, out_specs=[IN_VMEM] * 2
    )(lower, snapshots)
    parts = call(
        split_kernel, "raw_parts", [shape(rows, 2 * n, kind=BF16)] * 3, in_specs=[IN_VMEM] * 2, out_specs=[IN_VMEM] * 3
    )(lower, snapshots)
    others = received(theirs, "row", stages[0])
    others, parts = lax.optimization_barrier((others, parts))
    mine = total(mine, others)
    others, _ = lax.optimization_barrier((received(gram, "row", stages[-1]), mine))
    own_gram = summed_over(total(gram, others), "row", stages[0])
    lower_gram = passed_along(own_gram, "tm", 1)
    leaf = call(
        leaf_kernel,
        "leaf_roots",
        [
            shape(2, n, n),
            shape(2, 2, 2 * n, 2 * n, kind=BF16),
            shape(2, 2 * n, 4 * n, kind=BF16),
            shape(2, 2 * n, 2 * n, kind=BF16),
        ],
        in_specs=[IN_VMEM] * 3,
        out_specs=[IN_VMEM] * 4,
    )(lower_gram, own_gram, sketch)
    for bits in stages[:0:-1]:
        beside = leaf if bits == stages[1] else own_gram
        others, beside = lax.optimization_barrier((received(mine, "row", bits), beside))
        mine = total(mine, others)
        if bits == stages[1]:
            leaf = beside
    (theirs,) = received(mine, "row", stages[0])
    chunks = 4
    return tuple(
        call(
            merge_kernel,
            "merge",
            [shape(n, n), shape(rows, n)],
            in_specs=[IN_VMEM] * 10,
            out_specs=[ANYWHERE, ANYWHERE],
            scratch_shapes=[
                pltpu.VMEM((n, n), F32),
                pltpu.VMEM((rows, n), F32),
                pltpu.VMEM((rows, 2 * n), BF16),
                pltpu.VMEM((rows, 2 * n), BF16),
                pltpu.SemaphoreType.DMA,
                pltpu.SemaphoreType.DMA((chunks,)),
            ],
        )(mine, theirs, *leaf, *parts, snapshots)
    )


def product_t(left, right):
    return jnp.dot(left.T, right, precision=HIGHEST, preferred_element_type=F32)


def product(left, right):
    return jnp.dot(left, right, precision=HIGHEST, preferred_element_type=F32)


def inverse_root(matrix):
    frob_scale = jnp.sqrt(jnp.sum(matrix * matrix) + 1e-06)
    ident = jnp.eye(matrix.shape[0], dtype=matrix.dtype)
    y_iter = matrix / frob_scale
    z_iter = ident
    for repeat in range(NS_STEPS):
        middle = 1.5 * ident - 0.5 * product(z_iter, y_iter)
        y_iter = product(y_iter, middle)
        z_iter = product(middle, z_iter)
    return z_iter / jnp.sqrt(frob_scale)


def many_merges(snapshots, sketches, tree_depth):
    leaf_sum = row_sum(product_t(snapshots, snapshots))
    leaf_root = inverse_root(leaf_sum)
    mode_block = product(snapshots, leaf_root)
    own_gram = product_t(leaf_root, product(leaf_sum, leaf_root))
    for tree_level in range(tree_depth):
        sketch = sketches[tree_level]
        lower_block, lower_gram = passed_along((mode_block, own_gram), "tm", 1 << tree_level)
        cross_sum = row_sum(product_t(lower_block, mode_block))
        top_rows = jnp.concatenate([lower_gram, cross_sum], axis=1)
        bottom_rows = jnp.concatenate([cross_sum.T, own_gram], axis=1)
        gram_sum = jnp.concatenate([top_rows, bottom_rows], axis=0)
        joined = jnp.concatenate([lower_block, mode_block], axis=1)
        reduced = product(gram_sum, sketch)
        small = product_t(reduced, product(gram_sum, reduced))
        mixing = product(reduced, inverse_root(small))
        mode_block = product(joined, mixing)
        own_gram = product_t(mixing, product(gram_sum, mixing))
    coefficients = row_sum(product_t(mode_block, snapshots))
    deflated = snapshots - product(mode_block, coefficients)
    return coefficients, deflated


def body(snapshots, sketches):
    tree_depth = lax.axis_size("tm").bit_length() - 1
    row_count = lax.axis_size("row")
    if tree_depth == 1 and row_count >= 4 and row_count & (row_count - 1) == 0:
        return one_merge(snapshots, sketches[0])
    return many_merges(snapshots, sketches, tree_depth)


def solution(mesh):
    placed = (P("row", "tm"), P())
    return jax.shard_map(
        body, mesh=mesh, in_specs=placed, out_specs=(P(None, "tm"), P("row", "tm")), check_vma=False
    )
```
